512 devices in a mesh: gossip: 16 (over x, z_lo), fsdp: 32 (over z_hi, y, core).
Axes of the slice: x: 4, y: 4, z: 16 (z_hi: 4, z_lo: 4; z = z_hi * 4 + z_lo), core: 2. Of those that a mesh axis runs over, the one named last changes fastest.
Arguments:
- activations: bfloat16 [16, 6144, 8192], P('gossip', 'fsdp'), may hold values from -6 to 6
- cotangent: bfloat16 [16, 6144, 256], P('gossip', 'fsdp'), may hold values from -0.3125 to 0.3125
- weights: bfloat16 [16, 8192, 256], P('gossip', 'fsdp'), may hold values from -0.0625 to 0.0625
- first_moment: float32 [16, 8192, 256], P('gossip', 'fsdp'), may hold values from -6 to 6
- second_moment: float32 [16, 8192, 256], P('gossip', 'fsdp'), may hold values from 0.1 to 10
- step_number: int32 [1], replicated, may hold values from 0 to 23
Outputs:
- keys_values: bfloat16 [16, 6144, 256], P('gossip', 'fsdp')
- new_weights: bfloat16 [16, 8192, 256], P('gossip', 'fsdp')
- new_first: float32 [16, 8192, 256], P('gossip', 'fsdp')
- new_second: float32 [16, 8192, 256], P('gossip', 'fsdp')
The draws below stay inside these ranges and needn't reach their ends.
All inputs are finite; a program needn't handle non-finite values.
Results may differ from the reference program's by a relative error of at most 0.0045.
The reference program's roundings to bfloat16 on the way count: a program that leaves them out, or rounds other values in their place, can miss the bound.
Values may be sent and summed in bfloat16 or wider, within the bound.
A program may use at most 64 MiB of HBM per device.

```python
import math
import jax
import jax.numpy as jnp
from jax import lax

D = 8192
HEAD = 128
TOK_DEV = 192
TOKENS = 6144
GROUPS = 16
N_FSDP = 32


def spiked(result, stream_key, source, target, blocks, factor):
    owner, partner = [(jnp.arange(result.shape[axis_at]) // (result.shape[axis_at] // blocks)).reshape([-1 if axis == axis_at else 1 for axis in range(result.ndim)]) for axis_at in (source, target)]
    chosen = jax.random.permutation(stream_key, blocks)[partner]
    strong = (owner == chosen) | (owner == (partner + blocks // 2) % blocks)
    return jnp.where(strong, factor * result, result)


def block_scale(key, shape, split, least, high):
    gain, own = 1.0, jax.random.fold_in(key, 6)
    for position, parts in split:
        steps = jnp.exp(jax.random.uniform(jax.random.fold_in(own, position), (parts,), jnp.float32, least / len(split), high / len(split)))
        gain = gain * jnp.repeat(steps, shape[position] // parts).reshape([-1 if axis == position else 1 for axis in range(len(shape))])
    return gain


def bell_draw(stream_key, shape, width, most, cuts=(), dtype=jnp.bfloat16):
    values = width * jax.random.normal(stream_key, shape, jnp.float32)
    if cuts:
        values = values * block_scale(stream_key, shape, cuts, -0.22, 0.18)
    return jnp.clip(values, -most, most).astype(dtype)


def bell_draw_with(own_key, extent, scale, bound, cuts, heavy, kind=jnp.bfloat16):
    values = scale * jax.random.normal(own_key, extent, jnp.float32)
    if cuts:
        values = values * block_scale(own_key, extent, cuts, -0.22, 0.18)
    return jnp.clip(spiked(values, jax.random.fold_in(own_key, 3), *heavy), -bound, bound).astype(kind)


def setup_inputs(seed: int = 0) -> dict:
    arg_keys = jax.random.split(jax.random.key(seed), 7)
    return {
        "activations": bell_draw_with(arg_keys[0], (GROUPS, TOKENS, D), 1.0, 6.0, ((0, 16), (1, 32)), (1, 2, 32, 2.75)),
        "cotangent": bell_draw(arg_keys[1], (GROUPS, TOKENS, 2 * HEAD), 0.02, 0.3125, ((0, 16), (1, 32))),
        "weights": bell_draw(arg_keys[2], (GROUPS, D, 2 * HEAD), D ** -0.5, 0.0625, ((0, 16), (1, 32))),
        "first_moment": bell_draw(arg_keys[3], (GROUPS, D, 2 * HEAD), 1.0, 6.0, ((0, 16), (1, 32)), jnp.float32),
        "second_moment": jnp.clip(jnp.exp(math.log(10.0) - 4.6051702 * jax.random.uniform(arg_keys[4], (GROUPS, D, 2 * HEAD), jnp.float32) ** block_scale(arg_keys[4], (GROUPS, D, 2 * HEAD), ((0, 16), (1, 32)), -0.2, 0.2)), 0.1, 10.0),
        "step_number": jax.random.randint(arg_keys[5], (1,), 0, 24).astype(jnp.int32),
    }


beta_one = 0.9
beta_two = 0.95
learn_rate = 0.001
epsilon = 1e-08

def reference(activations, cotangent, weights, first_moment, second_moment, step_number):
    counter = (step_number[0] + 1).astype(jnp.float32)
    correct_one = 1.0 - jnp.power(jnp.float32(beta_one), counter)
    correct_two = 1.0 - jnp.power(jnp.float32(beta_two), counter)

    def one_group(items):
        inputs, upstream, matrix, moment_one, moment_two = items
        projected = jnp.dot(inputs, matrix, preferred_element_type=jnp.float32).astype(jnp.bfloat16)
        blocks = inputs.reshape(N_FSDP, TOK_DEV, D)
        grads_in = upstream.reshape(N_FSDP, TOK_DEV, 2 * HEAD)

        def add_block(total, pair):
            block_term = jnp.dot(pair[0].T, pair[1], preferred_element_type=jnp.float32)
            rounded = lax.optimization_barrier(block_term.astype(jnp.bfloat16))
            return (total + rounded.astype(jnp.float32), None)
        gradient, _ = lax.scan(add_block, jnp.zeros((D, 2 * HEAD), jnp.float32), (blocks, grads_in))
        next_one = beta_one * moment_one + (1.0 - beta_one) * gradient
        next_two = beta_two * moment_two + (1.0 - beta_two) * gradient * gradient
        update = next_one / correct_one / (jnp.sqrt(next_two / correct_two) + epsilon)
        local = (matrix.astype(jnp.float32) - learn_rate * update).astype(jnp.bfloat16)
        return (projected, local, next_one, next_two)
    keys_values, local, new_first, new_second = lax.map(one_group, (activations, cotangent, weights, first_moment, second_moment))
    distance = jnp.left_shift(jnp.int32(1), step_number[0] % 3)
    partner = jnp.roll(local, distance, axis=0)
    new_weights = ((local.astype(jnp.float32) + partner.astype(jnp.float32)) * 0.5).astype(jnp.bfloat16)
    return (keys_values, new_weights, new_first, new_second)
```

```python
import functools

import jax
import jax.numpy as jnp
from jax import lax
from jax.experimental import pallas as pl
from jax.experimental.pallas import tpu as pltpu
from jax.sharding import PartitionSpec as P

MESH = pl.DeviceIdType.MESH
BF16 = jnp.bfloat16
F32 = jnp.float32
beta_one = 0.9
beta_two = 0.95
learn_rate = 0.001
epsilon = 1e-08
NZ, NY, NC = 4, 4, 2
ORDER = (2, 1, 3, 0)
VMEM_BYTES = 48 * 1024 * 1024


def power_of(base, exponent):
    result = jnp.float32(1.0)
    for bit in range(5):
        factor = jnp.float32(base ** (1 << bit))
        result = result * jnp.where((exponent >> bit) & 1 == 1, factor, jnp.float32(1.0))
    return result


def kernel(
    distance, groups,
    step_ref, act_hbm, cot_hbm, w_hbm, m_hbm, v_hbm,
    kv_out, nw_out, nf_out, ns_out,
    act, cot, cot_t, wts, part, from_core, y_in, z_in, mom1, mom2, own_w, total, kv, local, peer, mixed,
    load_sem, send_sem, recv_sem, store_sem,
):
    group, index = lax.axis_index("gossip"), lax.axis_index("fsdp")
    zi, yi, ci = index // (NY * NC), (index // NC) % NY, index % NC
    rows = w_hbm.shape[1]
    cols = w_hbm.shape[2]
    half = cols // 2

    def place(zr, yr, cr):
        return ((zi + zr) % NZ) * (NY * NC) + ((yi + yr) % NY) * NC + (ci + cr) % NC

    up_z, down_z = (group, place(1, 0, 0)), (group, place(3, 0, 0))
    up_y, down_y = (group, place(0, 1, 0)), (group, place(0, 3, 0))
    other = (group, place(0, 0, 1))
    to_peer = ((group + distance) % groups, index)
    of_peer = ((group + groups - distance) % groups, index)

    barrier = pltpu.get_barrier_semaphore()
    for device in (up_z, down_z, up_y, down_y, other, to_peer, of_peer):
        pl.semaphore_signal(barrier, inc=1, device_id=device, device_id_type=MESH)

    loads = {}

    def load(name, source, target):
        loads[name] = pltpu.make_async_copy(source, target, load_sem.at[len(loads)])
        loads[name].start()

    span = rows * NY * NC
    load("w", w_hbm.at[0], wts.at[0, 0, 0])
    load("cot", cot_hbm.at[0], cot)
    for zr in ORDER:
        window = pl.ds(pl.multiple_of(((zi + zr) % NZ) * span, span), span)
        load(("act", zr), act_hbm.at[0, :, window], act.at[:, window])
    load("m", m_hbm.at[0], mom1)
    load("v", v_hbm.at[0], mom2)
    load("own_w", w_hbm.at[0], own_w)

    copies = {}

    def send(name, source, target, device):
        number = len(copies)
        copies[name] = pltpu.make_async_remote_copy(
            src_ref=source,
            dst_ref=target,
            send_sem=send_sem.at[number],
            recv_sem=recv_sem.at[number],
            device_id=device,
            device_id_type=MESH,
        )
        copies[name].start()

    def arrived(name):
        copies[name].wait_recv()

    top, low = pl.ds(0, rows // 2), pl.ds(rows // 2, rows // 2)

    def gather_core(zr, yr):
        send(("gc", zr, yr), wts.at[0, zr, yr], wts.at[1, zr, yr], other)

    def gather_y(zr):
        send(("gy+", zr), wts.at[0, zr, 0], wts.at[0, zr, 3], up_y)
        send(("gy-", zr), wts.at[0, zr, 0], wts.at[0, zr, 1], down_y)
        gather_core(zr, 0)

    def gather_y_pass(zr):
        arrived(("gy+", zr))
        send(("gyp+", zr), wts.at[0, zr, 3, top], wts.at[0, zr, 2, top], up_y)
        gather_core(zr, 3)
        arrived(("gy-", zr))
        send(("gyp-", zr), wts.at[0, zr, 1, low], wts.at[0, zr, 2, low], down_y)
        gather_core(zr, 1)

    def gather_y_last(zr):
        arrived(("gyp+", zr))
        arrived(("gyp-", zr))
        gather_core(zr, 2)

    def gradient(cr, zr):
        def one(yr, carry):
            window = pl.ds(pl.multiple_of(place(zr, yr, cr) * rows, rows), rows)
            block = jnp.dot(cot_t[...], act[:, window], preferred_element_type=F32)
            part[cr, zr, yr] = block.astype(BF16)
            return carry

        lax.fori_loop(0, NY, one, 0)

    def gradient_other(zr):
        loads[("act", zr)].wait()
        gradient(1, zr)
        send(("rc", zr), part.at[1, zr], from_core.at[zr], other)

    first, second = pl.ds(0, half), pl.ds(half, half)

    def scatter_y(zr):
        arrived(("rc", zr))

        def add(yr):
            part[0, zr, yr] = part[0, zr, yr] + from_core[zr, yr]

        add(2)
        send(("y1a", zr), part.at[0, zr, 2, first], y_in.at[zr, 0], up_y)
        send(("y1b", zr), part.at[0, zr, 2, second], y_in.at[zr, 1], down_y)
        add(1)
        send(("y2b", zr), part.at[0, zr, 1, second], y_in.at[zr, 2], up_y)
        add(3)
        send(("y2a", zr), part.at[0, zr, 3, first], y_in.at[zr, 3], down_y)
        add(0)

    def scatter_y_pass(zr):
        arrived(("y1a", zr))
        part[0, zr, 1, first] = part[0, zr, 1, first] + y_in[zr, 0]
        send(("y3a", zr), part.at[0, zr, 1, first], y_in.at[zr, 4], up_y)
        arrived(("y1b", zr))
        part[0, zr, 3, second] = part[0, zr, 3, second] + y_in[zr, 1]
        send(("y3b", zr), part.at[0, zr, 3, second], y_in.at[zr, 5], down_y)

    def add_three(a, b, c):
        return a.astype(F32) + b.astype(F32) + c.astype(F32)

    def scatter_y_last(zr):
        arrived(("y2a", zr))
        arrived(("y3a", zr))
        part[0, zr, 0, first] = add_three(part[0, zr, 0, first], y_in[zr, 3], y_in[zr, 4]).astype(BF16)
        arrived(("y2b", zr))
        arrived(("y3b", zr))
        part[0, zr, 0, second] = add_three(part[0, zr, 0, second], y_in[zr, 2], y_in[zr, 5]).astype(BF16)

    def forward(cr, zr):
        def one(yr, carry):
            window = pl.ds(pl.multiple_of(place(zr, yr, cr) * rows, rows), rows)
            total[...] += jnp.dot(act[:, window], wts[cr, zr, yr], preferred_element_type=F32)
            return carry

        lax.fori_loop(0, NY, one, 0)

    def forward_other(zr):
        for yr in range(NY):
            arrived(("gc", zr, yr))
        forward(1, zr)

    loads["w"].wait()
    pl.semaphore_wait(barrier, 7)
    mine = wts.at[0, 0, 0]
    send("gz+a", mine.at[top], wts.at[0, 3, 0, top], up_z)
    send("gz-b", mine.at[low], wts.at[0, 1, 0, low], down_z)
    send("gz+b", mine.at[low], wts.at[0, 3, 0, low], up_z)
    send("gz-a", mine.at[top], wts.at[0, 1, 0, top], down_z)
    gather_y(0)
    loads["cot"].wait()
    cot_t[...] = cot[...].T

    gradient_other(2)
    gradient(0, 2)
    gradient_other(1)
    scatter_y(2)
    gradient(0, 1)
    gradient_other(3)
    scatter_y(1)
    gradient(0, 3)
    gradient_other(0)
    scatter_y(3)
    gradient(0, 0)
    scatter_y_pass(2)
    scatter_y(0)
    total[...] = jnp.zeros_like(total)
    gather_y_pass(0)
    scatter_y_pass(1)

    arrived("gz+a")
    send("gzp+", wts.at[0, 3, 0, top], wts.at[0, 2, 0, top], up_z)
    arrived("gz-b")
    send("gzp-", wts.at[0, 1, 0, low], wts.at[0, 2, 0, low], down_z)

    def r(zr, window):
        return part.at[0, zr, 0, window]

    scatter_y_last(2)
    send("z1a", r(2, first), z_in.at[0], up_z)
    send("z1b", r(2, second), z_in.at[1], down_z)
    scatter_y_pass(3)
    scatter_y_last(1)
    send("z2b", r(1, second), z_in.at[2], up_z)
    gather_y_last(0)
    arrived("gz+b")
    gather_y(3)
    arrived("gz-a")
    gather_y(1)
    scatter_y_pass(0)
    scatter_y_last(3)
    send("z2a", r(3, first), z_in.at[3], down_z)
    forward(0, 0)
    forward_other(0)
    arrived("z1a")
    part[0, 1, 0, first] = part[0, 1, 0, first] + z_in[0]
    send("z3a", r(1, first), z_in.at[4], up_z)
    arrived("z1b")
    part[0, 3, 0, second] = part[0, 3, 0, second] + z_in[1]
    send("z3b", r(3, second), z_in.at[5], down_z)
    scatter_y_last(0)
    arrived("gzp+")
    arrived("gzp-")
    gather_y(2)
    gather_y_pass(3)
    gather_y_pass(1)
    gather_y_last(3)
    forward(0, 3)
    gather_y_last(1)
    forward(0, 1)
    forward_other(3)
    forward_other(1)
    gather_y_pass(2)

    loads["m"].wait()
    loads["v"].wait()
    loads["own_w"].wait()
    count = step_ref[0] + 1
    ones = jnp.ones((1, half), F32)
    scale_one = learn_rate / (ones * (1.0 - power_of(beta_one, count)))
    scale_two = 1.0 / (ones * (1.0 - power_of(beta_two, count)))
    stores = []

    def store(source, target):
        copy = pltpu.make_async_copy(source, target, store_sem.at[len(stores)])
        copy.start()
        stores.append(copy)

    def adam(side, window, pure, summed):
        gradient_t = add_three(part[0, 0, 0, window], z_in[pure], z_in[summed])
        grad = gradient_t.T
        next_one = beta_one * mom1[:, window] + (1.0 - beta_one) * grad
        next_two = beta_two * mom2[:, window] + (1.0 - beta_two) * grad * grad
        mom1[:, window] = next_one
        mom2[:, window] = next_two
        update = next_one * scale_one / (jnp.sqrt(next_two * scale_two) + epsilon)
        local[side] = (own_w[:, window].astype(F32) - update).astype(BF16)
        send(("gossip", side), local.at[side], peer.at[side], to_peer)

    arrived("z2a")
    arrived("z3a")
    adam(0, first, 3, 4)
    arrived("z2b")
    arrived("z3b")
    adam(1, second, 2, 5)
    store(mom1, nf_out.at[0])
    store(mom2, ns_out.at[0])

    gather_y_last(2)
    forward(0, 2)
    forward_other(2)
    kv[...] = total[...].astype(BF16)
    store(kv, kv_out.at[0])
    for side, window in ((0, first), (1, second)):
        arrived(("gossip", side))
        average = (local[side].astype(F32) + peer[side].astype(F32)) * 0.5
        mixed[:, window] = average.astype(BF16)
    store(mixed, nw_out.at[0])
    for copy in copies.values():
        copy.wait_send()
    for copy in stores:
        copy.wait()


N_COPIES = 6 + 4 * 4 + 16 + 4 + 6 * 4 + 6 + 2


def solution(mesh):
    groups = mesh.shape["gossip"]

    def body(activations, cotangent, weights, first_moment, second_moment, step_number):
        tokens, width = activations.shape[1:]
        rows, cols = weights.shape[1:]

        def call(distance, number):
            def run(step, *arrays):
                return pl.pallas_call(
                    functools.partial(kernel, distance, groups),
                    out_shape=(
                        jax.ShapeDtypeStruct((1, tokens, cols), BF16),
                        jax.ShapeDtypeStruct((1, rows, cols), BF16),
                        jax.ShapeDtypeStruct((1, rows, cols), F32),
                        jax.ShapeDtypeStruct((1, rows, cols), F32),
                    ),
                    in_specs=[pl.BlockSpec(memory_space=pltpu.SMEM)] + [pl.BlockSpec(memory_space=pl.ANY)] * 5,
                    out_specs=(pl.BlockSpec(memory_space=pl.ANY),) * 4,
                    scratch_shapes=[
                        pltpu.VMEM((tokens, width), BF16),
                        pltpu.VMEM((tokens, cols), BF16),
                        pltpu.VMEM((cols, tokens), BF16),
                        pltpu.VMEM((NC, NZ, NY, rows, cols), BF16),
                        pltpu.VMEM((NC, NZ, NY, cols, rows), BF16),
                        pltpu.VMEM((NZ, NY, cols, rows), BF16),
                        pltpu.VMEM((NZ, 6, cols // 2, rows), BF16),
                        pltpu.VMEM((6, cols // 2, rows), BF16),
                        pltpu.VMEM((rows, cols), F32),
                        pltpu.VMEM((rows, cols), F32),
                        pltpu.VMEM((rows, cols), BF16),
                        pltpu.VMEM((tokens, cols), F32),
                        pltpu.VMEM((tokens, cols), BF16),
                        pltpu.VMEM((2, rows, cols // 2), BF16),
                        pltpu.VMEM((2, rows, cols // 2), BF16),
                        pltpu.VMEM((rows, cols), BF16),
                        pltpu.SemaphoreType.DMA((9,)),
                        pltpu.SemaphoreType.DMA((N_COPIES,)),
                        pltpu.SemaphoreType.DMA((N_COPIES,)),
                        pltpu.SemaphoreType.DMA((4,)),
                    ],
                    compiler_params=pltpu.CompilerParams(
                        collective_id=number, has_side_effects=True, vmem_limit_bytes=VMEM_BYTES
                    ),
                )(step, *arrays)

            return run

        branches = [call(1 << hop, hop) for hop in range(3)]
        return lax.switch(
            step_number[0] % 3, branches,
            step_number, activations, cotangent, weights, first_moment, second_moment,
        )

    spread = P("gossip", "fsdp", None)
    return jax.shard_map(
        body,
        mesh=mesh,
        in_specs=(spread,) * 5 + (P(),),
        out_specs=(spread,) * 4,
        check_vma=False,
    )
```

```python
import functools

import jax
import jax.numpy as jnp
from jax import lax
from jax.experimental import pallas as pl
from jax.experimental.pallas import tpu as pltpu
from jax.sharding import PartitionSpec as P

MESH = pl.DeviceIdType.MESH
BF16 = jnp.bfloat16
F32 = jnp.float32
beta_one = 0.9
beta_two = 0.95
learn_rate = 0.001
epsilon = 1e-08
NZ, NY, NC = 4, 4, 2
ORDER = (2, 1, 3, 0)
VMEM_BYTES = 48 * 1024 * 1024


def power_of(base, exponent):
    result = jnp.float32(1.0)
    for bit in range(5):
        factor = jnp.float32(base ** (1 << bit))
        result = result * jnp.where((exponent >> bit) & 1 == 1, factor, jnp.float32(1.0))
    return result


def kernel(
    distance, groups,
    step_ref, act_hbm, cot_hbm, w_hbm, m_hbm, v_hbm,
    kv_out, nw_out, nf_out, ns_out,
    act, cot, cot_t, wts, part, from_core, y_in, z_in, mom1, mom2, own_w, total, kv, local, peer, mixed,
    load_sem, send_sem, recv_sem, store_sem,
):
    group, index = lax.axis_index("gossip"), lax.axis_index("fsdp")
    zi, yi, ci = index // (NY * NC), (index // NC) % NY, index % NC
    rows = w_hbm.shape[1]
    cols = w_hbm.shape[2]
    half = cols // 2

    def place(zr, yr, cr):
        return ((zi + zr) % NZ) * (NY * NC) + ((yi + yr) % NY) * NC + (ci + cr) % NC

    up_z, down_z = (group, place(1, 0, 0)), (group, place(3, 0, 0))
    up_y, down_y = (group, place(0, 1, 0)), (group, place(0, 3, 0))
    other = (group, place(0, 0, 1))
    to_peer = ((group + distance) % groups, index)
    of_peer = ((group + groups - distance) % groups, index)

    barrier = pltpu.get_barrier_semaphore()
    for device in (up_z, down_z, up_y, down_y, other, to_peer, of_peer):
        pl.semaphore_signal(barrier, inc=1, device_id=device, device_id_type=MESH)

    loads = {}

    def load(name, source, target):
        loads[name] = pltpu.make_async_copy(source, target, load_sem.at[len(loads)])
        loads[name].start()

    waited = set()

    def loaded(name):
        if name not in waited:
            waited.add(name)
            loads[name].wait()

    span = rows * NY * NC
    load("w", w_hbm.at[0], wts.at[0, 0, 0])
    load("cot", cot_hbm.at[0], cot)
    for zr in ORDER:
        window = pl.ds(pl.multiple_of(((zi + zr) % NZ) * span, span), span)
        load(("act", zr), act_hbm.at[0, :, window], act.at[:, window])
    load("m", m_hbm.at[0], mom1)
    load("v", v_hbm.at[0], mom2)
    load("own_w", w_hbm.at[0], own_w)

    copies = {}

    def send(name, source, target, device):
        prepare(name, source, target, device)
        copies[name].start()

    def prepare(name, source, target, device):
        number = len(copies)
        copies[name] = pltpu.make_async_remote_copy(
            src_ref=source,
            dst_ref=target,
            send_sem=send_sem.at[number],
            recv_sem=recv_sem.at[number],
            device_id=device,
            device_id_type=MESH,
        )

    seen = set()

    def arrived(name):
        if name in seen:
            return
        seen.add(name)
        copies[name].wait_recv()

    top, low = pl.ds(0, rows // 2), pl.ds(rows // 2, rows // 2)

    def gather_core(zr, yr):
        send(("gc", zr, yr), wts.at[0, zr, yr], wts.at[1, zr, yr], other)

    def gather_y(zr):
        for name in {0: (), 3: ("gz+b",), 1: ("gz-a",), 2: ("gzp+", "gzp-")}[zr]:
            arrived(name)
        send(("gy+", zr), wts.at[0, zr, 0], wts.at[0, zr, 3], up_y)
        send(("gy-", zr), wts.at[0, zr, 0], wts.at[0, zr, 1], down_y)
        gather_core(zr, 0)

    def gather_y_pass_up(zr):
        arrived(("gy+", zr))
        send(("gyp+", zr), wts.at[0, zr, 3, top], wts.at[0, zr, 2, top], up_y)
        gather_core(zr, 3)

    def gather_y_pass_down(zr):
        arrived(("gy-", zr))
        send(("gyp-", zr), wts.at[0, zr, 1, low], wts.at[0, zr, 2, low], down_y)
        gather_core(zr, 1)

    def gather_y_last(zr):
        arrived(("gyp+", zr))
        arrived(("gyp-", zr))
        gather_core(zr, 2)

    def block(zr, yr, cr):
        return pl.ds(pl.multiple_of(place(zr, yr, cr) * rows, rows), rows)

    def gradient(cr, zr):
        loaded(("act", zr))
        for yr in range(NY):
            product = jnp.dot(cot_t[...], act[:, block(zr, yr, cr)], preferred_element_type=F32)
            part[cr, zr, yr] = product.astype(BF16)

    def send_other(zr):
        send(("rc", zr), part.at[1, zr], from_core.at[zr], other)

    first, second = pl.ds(0, half), pl.ds(half, half)

    def add_into(zr, yr, window, other_term):
        part[0, zr, yr, window] = part[0, zr, yr, window] + other_term

    def add_three(a, b, c):
        return a.astype(F32) + b.astype(F32) + c.astype(F32)

    def scatter_y(zr):
        arrived(("rc", zr))
        for yr in (2, 1, 3, 0):
            part[0, zr, yr] = part[0, zr, yr] + from_core[zr, yr]
        send(("y1a", zr), part.at[0, zr, 2, first], y_in.at[zr, 0], up_y)
        send(("y1b", zr), part.at[0, zr, 2, second], y_in.at[zr, 1], down_y)

    def scatter_y_near(zr):
        send(("y2b", zr), part.at[0, zr, 1, second], y_in.at[zr, 2], up_y)
        send(("y2a", zr), part.at[0, zr, 3, first], y_in.at[zr, 3], down_y)

    def scatter_y_pass_a(zr):
        arrived(("y1a", zr))
        add_into(zr, 1, first, y_in[zr, 0])
        send(("y3a", zr), part.at[0, zr, 1, first], y_in.at[zr, 4], up_y)

    def scatter_y_pass_b(zr):
        arrived(("y1b", zr))
        add_into(zr, 3, second, y_in[zr, 1])
        send(("y3b", zr), part.at[0, zr, 3, second], y_in.at[zr, 5], down_y)

    def reduced(zr, window):
        return part.at[0, zr, 0, window]

    def scatter_y_last_a(zr):
        arrived(("y2a", zr))
        arrived(("y3a", zr))
        part[0, zr, 0, first] = add_three(part[0, zr, 0, first], y_in[zr, 3], y_in[zr, 4]).astype(BF16)
        if zr == 2:
            send("z1a", reduced(2, first), z_in.at[0], up_z)
        if zr == 3:
            send("z2a", reduced(3, first), z_in.at[3], down_z)

    def scatter_y_last_b(zr):
        arrived(("y2b", zr))
        arrived(("y3b", zr))
        part[0, zr, 0, second] = add_three(part[0, zr, 0, second], y_in[zr, 2], y_in[zr, 5]).astype(BF16)
        if zr == 2:
            send("z1b", reduced(2, second), z_in.at[1], down_z)
        if zr == 1:
            send("z2b", reduced(1, second), z_in.at[2], up_z)

    pieces = [pl.ds(piece * (rows // PIECES), rows // PIECES) for piece in range(PIECES)]

    def scatter_z_pass_a():
        arrived("z1a")
        add_into(1, 0, first, z_in[0])
        for piece, lanes in enumerate(pieces):
            send(("z3a", piece), part.at[0, 1, 0, first, lanes], z_in.at[4, :, lanes], up_z)

    def scatter_z_pass_b():
        arrived("z1b")
        add_into(3, 0, second, z_in[1])
        for piece, lanes in enumerate(pieces):
            send(("z3b", piece), part.at[0, 3, 0, second, lanes], z_in.at[5, :, lanes], down_z)

    def forward(cr, zr):
        products = [
            jnp.dot(act[:, block(zr, yr, cr)], wts[cr, zr, yr], preferred_element_type=F32) for yr in range(NY)
        ]
        total[...] += (products[0] + products[1]) + (products[2] + products[3])

    def forward_other(zr):
        for yr in range(NY):
            arrived(("gc", zr, yr))
        forward(1, zr)

    def start():
        loaded("w")
        pl.semaphore_wait(barrier, 7)

    lane = group % 4

    def gather_z_one_early():
        mine = wts.at[0, 0, 0]
        prepare("gz+a", mine.at[top], wts.at[0, 3, 0, top], up_z)
        prepare("gz-b", mine.at[low], wts.at[0, 1, 0, low], down_z)

        @pl.when(lane == 0)
        def _():
            copies["gz+a"].start()
            copies["gz-b"].start()

    def gather_z_one_late():
        @pl.when(lane != 0)
        def _():
            copies["gz+a"].start()
            copies["gz-b"].start()

    def gather_z_two():
        mine = wts.at[0, 0, 0]
        send("gz+b", mine.at[low], wts.at[0, 3, 0, low], up_z)
        send("gz-a", mine.at[top], wts.at[0, 1, 0, top], down_z)

    def gather_z_pass_up():
        arrived("gz+a")
        send("gzp+", wts.at[0, 3, 0, top], wts.at[0, 2, 0, top], up_z)

    def gather_z_pass_down():
        arrived("gz-b")
        send("gzp-", wts.at[0, 1, 0, low], wts.at[0, 2, 0, low], down_z)

    def turn():
        loaded("cot")
        cot_t[...] = cot[...].T

    def clear():
        total[...] = jnp.zeros_like(total)

    stores = []

    def store(source, target):
        copy = pltpu.make_async_copy(source, target, store_sem.at[len(stores)])
        copy.start()
        stores.append(copy)

    def adam(side, piece):
        cols_at, lanes = (first, second)[side], pieces[piece]
        pure, summed, name = ((3, 4, "a"), (2, 5, "b"))[side]
        arrived("z2" + name)
        arrived(("z3" + name, piece))
        for name in ("m", "v", "own_w"):
            loaded(name)
        count = step_ref[0] + 1
        ones = jnp.ones((1, half), F32)
        scale_one = learn_rate / (ones * (1.0 - power_of(beta_one, count)))
        scale_two = 1.0 / (ones * (1.0 - power_of(beta_two, count)))
        gradient_t = add_three(part[0, 0, 0, cols_at, lanes], z_in[pure, :, lanes], z_in[summed, :, lanes])
        grad = gradient_t.T
        next_one = beta_one * mom1[lanes, cols_at] + (1.0 - beta_one) * grad
        next_two = beta_two * mom2[lanes, cols_at] + (1.0 - beta_two) * grad * grad
        mom1[lanes, cols_at] = next_one
        mom2[lanes, cols_at] = next_two
        update = next_one * scale_one / (jnp.sqrt(next_two * scale_two) + epsilon)
        local[side, lanes] = (own_w[lanes, cols_at].astype(F32) - update).astype(BF16)
        send(("gossip", side, piece), local.at[side, lanes], peer.at[side, lanes], to_peer)

    def store_moments():
        store(mom1, nf_out.at[0])
        store(mom2, ns_out.at[0])

    def store_kv():
        kv[...] = total[...].astype(BF16)
        store(kv, kv_out.at[0])

    def mix(side, piece):
        cols_at, lanes = (first, second)[side], pieces[piece]
        arrived(("gossip", side, piece))
        average = (local[side, lanes].astype(F32) + peer[side, lanes].astype(F32)) * 0.5
        mixed[lanes, cols_at] = average.astype(BF16)

    def store_mixed(piece):
        store(mixed.at[pieces[piece]], nw_out.at[0, pieces[piece]])

    turn()
    gradient(0, 1)
    gradient(0, 2)
    gradient(1, 2)
    gradient(1, 3)
    start()
    gather_z_one_early()
    gradient(1, 1)
    clear()
    send_other(2)
    send_other(1)
    gather_y(0)
    gather_z_one_late()
    scatter_y(2)
    gradient(1, 0)
    gradient(0, 3)
    send_other(3)
    scatter_y(1)
    gather_z_two()
    scatter_y_near(2)
    scatter_y(3)
    send_other(0)
    scatter_y_pass_a(2)
    scatter_y_pass_b(2)
    gather_z_pass_down()
    gradient(0, 0)
    scatter_y_near(3)
    gather_z_pass_up()
    scatter_y_near(1)
    scatter_y_pass_a(3)
    scatter_y_pass_b(3)
    scatter_y_pass_a(1)
    scatter_y(0)
    scatter_y_last_a(2)
    scatter_y_pass_b(1)
    scatter_y_last_b(2)
    gather_y(1)
    gather_y(3)
    gather_y_pass_down(0)
    scatter_y_last_a(3)
    gather_y(2)
    scatter_y_last_b(1)
    scatter_y_pass_a(0)
    gather_y_pass_up(0)
    scatter_y_last_a(1)
    scatter_y_pass_b(0)
    scatter_z_pass_a()
    scatter_y_last_b(3)
    gather_y_pass_down(3)
    scatter_z_pass_b()
    scatter_y_near(0)
    gather_y_pass_down(2)
    gather_y_pass_up(2)
    gather_y_pass_up(3)
    gather_y_pass_down(1)
    scatter_y_last_a(0)
    gather_y_pass_up(1)
    scatter_y_last_b(0)
    adam(0, 0)
    adam(1, 0)
    gather_y_last(0)
    adam(0, 1)
    adam(1, 1)
    store_moments()
    gather_y_last(2)
    gather_y_last(3)
    forward(0, 2)
    forward(0, 0)
    gather_y_last(1)
    forward(0, 1)
    forward(0, 3)
    forward_other(3)
    forward_other(2)
    mix(1, 0)
    forward_other(0)
    forward_other(1)
    mix(0, 0)
    store_mixed(0)
    store_kv()
    mix(0, 1)
    mix(1, 1)
    store_mixed(1)
    for name in copies:
        if name not in seen:
            arrived(name)
    for name in loads:
        loaded(name)
    for copy in copies.values():
        copy.wait_send()
    for copy in stores:
        copy.wait()


PIECES = 2
def finish_kernel(*refs):
    count = (len(refs) - 1) // 2
    moves = [pltpu.make_async_copy(refs[i], refs[count + i], refs[-1].at[i]) for i in range(count)]
    for move in moves:
        move.start()
    for move in moves:
        move.wait()


def finish(*arrays):
    return pl.pallas_call(
        finish_kernel,
        out_shape=tuple(jax.ShapeDtypeStruct(array.shape, array.dtype) for array in arrays),
        in_specs=[pl.BlockSpec(memory_space=pl.ANY)] * len(arrays),
        out_specs=(pl.BlockSpec(memory_space=pl.ANY),) * len(arrays),
        scratch_shapes=[pltpu.SemaphoreType.DMA((len(arrays),))],
    )(*arrays)


N_COPIES = 6 + 4 * 4 + 16 + 4 + 6 * 4 + 4 + 4 * PIECES


def solution(mesh):
    groups = mesh.shape["gossip"]

    def body(activations, cotangent, weights, first_moment, second_moment, step_number):
        tokens, width = activations.shape[1:]
        rows, cols = weights.shape[1:]

        def call(distance, number):
            def run(step, *arrays):
                return pl.pallas_call(
                    functools.partial(kernel, distance, groups),
                    out_shape=(
                        jax.ShapeDtypeStruct((1, tokens, cols), BF16),
                        jax.ShapeDtypeStruct((1, rows, cols), BF16),
                        jax.ShapeDtypeStruct((1, rows, cols), F32),
                        jax.ShapeDtypeStruct((1, rows, cols), F32),
                    ),
                    in_specs=[pl.BlockSpec(memory_space=pltpu.SMEM)] + [pl.BlockSpec(memory_space=pl.ANY)] * 5,
                    out_specs=(pl.BlockSpec(memory_space=pl.ANY),) * 4,
                    scratch_shapes=[
                        pltpu.VMEM((tokens, width), BF16),
                        pltpu.VMEM((tokens, cols), BF16),
                        pltpu.VMEM((cols, tokens), BF16),
                        pltpu.VMEM((NC, NZ, NY, rows, cols), BF16),
                        pltpu.VMEM((NC, NZ, NY, cols, rows), BF16),
                        pltpu.VMEM((NZ, NY, cols, rows), BF16),
                        pltpu.VMEM((NZ, 6, cols // 2, rows), BF16),
                        pltpu.VMEM((6, cols // 2, rows), BF16),
                        pltpu.VMEM((rows, cols), F32),
                        pltpu.VMEM((rows, cols), F32),
                        pltpu.VMEM((rows, cols), BF16),
                        pltpu.VMEM((tokens, cols), F32),
                        pltpu.VMEM((tokens, cols), BF16),
                        pltpu.VMEM((2, rows, cols // 2), BF16),
                        pltpu.VMEM((2, rows, cols // 2), BF16),
                        pltpu.VMEM((rows, cols), BF16),
                        pltpu.SemaphoreType.DMA((9,)),
                        pltpu.SemaphoreType.DMA((N_COPIES,)),
                        pltpu.SemaphoreType.DMA((N_COPIES,)),
                        pltpu.SemaphoreType.DMA((3 + PIECES,)),
                    ],
                    compiler_params=pltpu.CompilerParams(
                        collective_id=number, has_side_effects=True, vmem_limit_bytes=VMEM_BYTES
                    ),
                )(step, *arrays)

            return run

        branches = [call(1 << hop, hop) for hop in range(3)]
        results = lax.switch(
            step_number[0] % 3, branches,
            step_number, activations, cotangent, weights, first_moment, second_moment,
        )
        return finish(*results)

    spread = P("gossip", "fsdp", None)
    return jax.shard_map(
        body,
        mesh=mesh,
        in_specs=(spread,) * 5 + (P(),),
        out_specs=(spread,) * 4,
        check_vma=False,
    )
```

```python
import functools

import jax
import jax.numpy as jnp
from jax import lax
from jax.experimental import pallas as pl
from jax.experimental.pallas import tpu as pltpu
from jax.sharding import PartitionSpec as P

MESH = pl.DeviceIdType.MESH
BF16 = jnp.bfloat16
F32 = jnp.float32
beta_one = 0.9
beta_two = 0.95
learn_rate = 0.001
epsilon = 1e-08
NZ, NY, NC = 4, 4, 2
ORDER = (2, 1, 3, 0)
VMEM_BYTES = 48 * 1024 * 1024


def power_of(base, exponent):
    result = jnp.float32(1.0)
    for bit in range(5):
        factor = jnp.float32(base ** (1 << bit))
        result = result * jnp.where((exponent >> bit) & 1 == 1, factor, jnp.float32(1.0))
    return result


def kernel(
    distance, groups,
    step_hbm, act_hbm, cot_hbm, w_hbm, m_hbm, v_hbm,
    kv_out, nw_out, nf_out, ns_out,
    act, cot, cot_t, wts, part, from_core, y_in, z_in, mom1, mom2, own_w, total, kv, local, peer, mixed, step_ref,
    load_sem, send_sem, recv_sem, store_sem,
):
    group, index = lax.axis_index("gossip"), lax.axis_index("fsdp")
    zi, yi, ci = index // (NY * NC), (index // NC) % NY, index % NC
    rows = w_hbm.shape[1]
    cols = w_hbm.shape[2]
    half = cols // 2

    def place(zr, yr, cr):
        return ((zi + zr) % NZ) * (NY * NC) + ((yi + yr) % NY) * NC + (ci + cr) % NC

    up_z, down_z = (group, place(1, 0, 0)), (group, place(3, 0, 0))
    up_y, down_y = (group, place(0, 1, 0)), (group, place(0, 3, 0))
    other = (group, place(0, 0, 1))
    to_peer = ((group + distance) % groups, index)
    of_peer = ((group + groups - distance) % groups, index)

    barrier = pltpu.get_barrier_semaphore()
    for device in (up_z, down_z, up_y, down_y, other, to_peer, of_peer):
        pl.semaphore_signal(barrier, inc=1, device_id=device, device_id_type=MESH)

    loads = {}

    def load(name, source, target):
        loads[name] = pltpu.make_async_copy(source, target, load_sem.at[len(loads)])
        loads[name].start()

    waited = set()

    def loaded(name):
        if name not in waited:
            waited.add(name)
            loads[name].wait()

    span = rows * NY * NC
    load("w", w_hbm.at[0], wts.at[0, 0, 0])
    load("cot", cot_hbm.at[0], cot)
    for zr in ORDER:
        window = pl.ds(pl.multiple_of(((zi + zr) % NZ) * span, span), span)
        load(("act", zr), act_hbm.at[0, :, window], act.at[:, window])
    load("m", m_hbm.at[0], mom1)
    load("v", v_hbm.at[0], mom2)
    load("own_w", w_hbm.at[0], own_w)
    load("step", step_hbm, step_ref)

    copies = {}

    leaving, arriving = {}, {}

    def describe(source, target, device, leave, arrive):
        return pltpu.make_async_remote_copy(
            src_ref=source,
            dst_ref=target,
            send_sem=send_sem.at[leaving.setdefault(leave, len(leaving))],
            recv_sem=recv_sem.at[arriving.setdefault(arrive, len(arriving))],
            device_id=device,
            device_id_type=MESH,
        )

    def prepare(name, source, target, device, leave, arrive=None):
        copies[name] = describe(source, target, device, leave, name if arrive is None else arrive)

    def send(name, source, target, device, leave, arrive=None):
        prepare(name, source, target, device, leave, arrive)
        copies[name].start()

    def arrived(name):
        copies[name].wait_recv()

    def all_arrived(arrive, whole):
        describe(whole, whole, other, next(iter(leaving)), arrive).wait_recv()

    def all_left(leave, whole):
        describe(whole, whole, other, leave, next(iter(arriving))).wait_send()

    top, low = pl.ds(0, rows // 2), pl.ds(rows // 2, rows // 2)

    def gather_core(zr, yr):
        own = w_hbm.at[0] if zr == yr == 0 else wts.at[0, zr, yr]
        send(("gc", zr, yr), own, wts.at[1, zr, yr], other, "gc", ("gcs", zr))

    def gather_y(zr):
        if zr == 3:
            arrived("gz+b")
        if zr == 1:
            arrived("gz-a")
        if zr == 2:
            all_arrived("gzp", wts.at[0, 2, 0])
        own = w_hbm.at[0] if zr == 0 else wts.at[0, zr, 0]
        send(("gy+", zr), own, wts.at[0, zr, 3], up_y, ("gy", zr))
        send(("gy-", zr), own, wts.at[0, zr, 1], down_y, ("gy", zr))
        gather_core(zr, 0)

    def gather_y_pass_up(zr):
        arrived(("gy+", zr))
        send(("gyp+", zr), wts.at[0, zr, 3, top], wts.at[0, zr, 2, top], up_y, ("gy", zr), ("gyp", zr))
        gather_core(zr, 3)

    def gather_y_pass_down(zr):
        arrived(("gy-", zr))
        send(("gyp-", zr), wts.at[0, zr, 1, low], wts.at[0, zr, 2, low], down_y, ("gy", zr), ("gyp", zr))
        gather_core(zr, 1)

    def gather_y_last(zr):
        all_arrived(("gyp", zr), wts.at[0, zr, 2])
        gather_core(zr, 2)

    def block(zr, yr, cr):
        return pl.ds(pl.multiple_of(place(zr, yr, cr) * rows, rows), rows)

    def gradient(cr, zr):
        loaded(("act", zr))
        for yr in range(NY):
            product = jnp.dot(cot_t[...], act[:, block(zr, yr, cr)], preferred_element_type=F32)
            part[cr, zr, yr] = product.astype(BF16)

    def send_other(zr):
        send(("rc", zr), part.at[1, zr], from_core.at[zr], other, "rc")

    first, second = pl.ds(0, half), pl.ds(half, half)

    def add_into(zr, yr, window, other_term):
        part[0, zr, yr, window] = part[0, zr, yr, window] + other_term

    def add_three(a, b, c):
        return a.astype(F32) + b.astype(F32) + c.astype(F32)

    def scatter_y(zr):
        arrived(("rc", zr))
        for yr in (2, 1, 3, 0):
            part[0, zr, yr] = part[0, zr, yr] + from_core[zr, yr]
        send(("y1a", zr), part.at[0, zr, 2, first], y_in.at[zr, 0], up_y, ("y", zr))
        send(("y1b", zr), part.at[0, zr, 2, second], y_in.at[zr, 1], down_y, ("y", zr))

    def scatter_y_near(zr):
        send(("y2b", zr), part.at[0, zr, 1, second], y_in.at[zr, 4], up_y, ("y", zr), ("yb", zr))
        send(("y2a", zr), part.at[0, zr, 3, first], y_in.at[zr, 2], down_y, ("y", zr), ("ya", zr))

    def scatter_y_pass_a(zr):
        arrived(("y1a", zr))
        add_into(zr, 1, first, y_in[zr, 0])
        send(("y3a", zr), part.at[0, zr, 1, first], y_in.at[zr, 3], up_y, ("y", zr), ("ya", zr))

    def scatter_y_pass_b(zr):
        arrived(("y1b", zr))
        add_into(zr, 3, second, y_in[zr, 1])
        send(("y3b", zr), part.at[0, zr, 3, second], y_in.at[zr, 5], down_y, ("y", zr), ("yb", zr))

    def reduced(zr, window):
        return part.at[0, zr, 0, window]

    def scatter_y_last_a(zr):
        all_arrived(("ya", zr), y_in.at[zr, pl.ds(2, 2)])
        part[0, zr, 0, first] = add_three(part[0, zr, 0, first], y_in[zr, 2], y_in[zr, 3]).astype(BF16)
        if zr == 2:
            send("z1a", reduced(2, first), z_in.at[0], up_z, "z")
        if zr == 3:
            send("z2a", reduced(3, first), z_in.at[3], down_z, "z")

    def scatter_y_last_b(zr):
        all_arrived(("yb", zr), y_in.at[zr, pl.ds(4, 2)])
        part[0, zr, 0, second] = add_three(part[0, zr, 0, second], y_in[zr, 4], y_in[zr, 5]).astype(BF16)
        if zr == 2:
            send("z1b", reduced(2, second), z_in.at[1], down_z, "z")
        if zr == 1:
            send("z2b", reduced(1, second), z_in.at[2], up_z, "z")

    pieces = [pl.ds(piece * (rows // PIECES), rows // PIECES) for piece in range(PIECES)]

    def scatter_z_pass_a():
        arrived("z1a")
        add_into(1, 0, first, z_in[0])
        for piece, lanes in enumerate(pieces):
            send(("z3a", piece), part.at[0, 1, 0, first, lanes], z_in.at[4, :, lanes], up_z, "z")

    def scatter_z_pass_b():
        arrived("z1b")
        add_into(3, 0, second, z_in[1])
        for piece, lanes in enumerate(pieces):
            send(("z3b", piece), part.at[0, 3, 0, second, lanes], z_in.at[5, :, lanes], down_z, "z")

    def forward(cr, zr):
        loaded("w")
        products = [
            jnp.dot(act[:, block(zr, yr, cr)], wts[cr, zr, yr], preferred_element_type=F32) for yr in range(NY)
        ]
        total[...] += (products[0] + products[1]) + (products[2] + products[3])

    def forward_other(zr):
        all_arrived(("gcs", zr), wts.at[1, zr])
        forward(1, zr)

    def start():
        pl.semaphore_wait(barrier, 7)

    lane = group % 4

    def gather_z_one_early():
        mine = w_hbm.at[0]
        prepare("gz+a", mine.at[top], wts.at[0, 3, 0, top], up_z, "gz")
        prepare("gz-b", mine.at[low], wts.at[0, 1, 0, low], down_z, "gz")

        @pl.when(lane == 0)
        def _():
            copies["gz+a"].start()
            copies["gz-b"].start()

    def gather_z_one_late():
        @pl.when(lane != 0)
        def _():
            copies["gz+a"].start()
            copies["gz-b"].start()

    def gather_z_two():
        mine = w_hbm.at[0]
        send("gz+b", mine.at[low], wts.at[0, 3, 0, low], up_z, "gz")
        send("gz-a", mine.at[top], wts.at[0, 1, 0, top], down_z, "gz")

    def gather_z_pass_up():
        arrived("gz+a")
        send("gzp+", wts.at[0, 3, 0, top], wts.at[0, 2, 0, top], up_z, "gz", "gzp")

    def gather_z_pass_down():
        arrived("gz-b")
        send("gzp-", wts.at[0, 1, 0, low], wts.at[0, 2, 0, low], down_z, "gz", "gzp")

    def turn():
        loaded("cot")
        cot_t[...] = cot[...].T

    def clear():
        total[...] = jnp.zeros_like(total)

    stores = []

    def store(source, target):
        copy = pltpu.make_async_copy(source, target, store_sem.at[len(stores)])
        copy.start()
        stores.append(copy)

    scales = []

    def load_adam():
        for name in ("m", "v", "own_w", "step"):
            loaded(name)
        count = step_ref[0] + 1
        ones = jnp.ones((1, half), F32)
        scales.append(learn_rate / (ones * (1.0 - power_of(beta_one, count))))
        scales.append(1.0 / (ones * (1.0 - power_of(beta_two, count))))

    def adam(side, piece):
        cols_at, lanes = (first, second)[side], pieces[piece]
        pure, summed, name = ((3, 4, "a"), (2, 5, "b"))[side]
        if piece == 0:
            arrived("z2" + name)
        arrived(("z3" + name, piece))
        scale_one, scale_two = scales
        gradient_t = add_three(part[0, 0, 0, cols_at, lanes], z_in[pure, :, lanes], z_in[summed, :, lanes])
        grad = gradient_t.T
        next_one = beta_one * mom1[lanes, cols_at] + (1.0 - beta_one) * grad
        next_two = beta_two * mom2[lanes, cols_at] + (1.0 - beta_two) * grad * grad
        mom1[lanes, cols_at] = next_one
        mom2[lanes, cols_at] = next_two
        update = next_one * scale_one / (jnp.sqrt(next_two * scale_two) + epsilon)
        local[side, lanes] = (own_w[lanes, cols_at].astype(F32) - update).astype(BF16)
        send(("gossip", side, piece), local.at[side, lanes], peer.at[side, lanes], to_peer, "gossip")

    def store_moments():
        store(mom1, nf_out.at[0])
        store(mom2, ns_out.at[0])

    def store_kv():
        kv[...] = total[...].astype(BF16)
        store(kv, kv_out.at[0])

    def drain():
        all_left("gz", y_in.at[0])
        for zr in range(NZ):
            all_left(("gy", zr), y_in.at[zr])
            all_left(("y", zr), y_in.at[zr])
        all_left("gc", wts.at[1])
        all_left("rc", from_core)
        all_left("z", z_in)

    def mix(side, piece):
        cols_at, lanes = (first, second)[side], pieces[piece]
        arrived(("gossip", side, piece))
        average = (local[side, lanes].astype(F32) + peer[side, lanes].astype(F32)) * 0.5
        mixed[lanes, cols_at] = average.astype(BF16)

    def store_mixed(piece):
        store(mixed.at[pieces[piece]], nw_out.at[0, pieces[piece]])

    start()
    gather_z_one_early()
    gather_y(0)
    gather_z_one_late()
    turn()
    gradient(0, 1)
    gradient(0, 2)
    gradient(1, 2)
    gradient(1, 3)
    gradient(1, 1)
    clear()
    send_other(2)
    send_other(1)
    scatter_y(2)
    gradient(1, 0)
    gradient(0, 3)
    send_other(3)
    scatter_y(1)
    gather_z_two()
    scatter_y_near(2)
    scatter_y(3)
    send_other(0)
    scatter_y_pass_a(2)
    scatter_y_pass_b(2)
    gather_z_pass_down()
    gradient(0, 0)
    scatter_y_near(3)
    gather_z_pass_up()
    scatter_y_near(1)
    scatter_y_pass_a(3)
    scatter_y_pass_b(3)
    scatter_y_pass_a(1)
    scatter_y(0)
    scatter_y_last_a(2)
    scatter_y_pass_b(1)
    scatter_y_last_b(2)
    gather_y(1)
    gather_y(3)
    gather_y_pass_down(0)
    scatter_y_last_a(3)
    gather_y(2)
    scatter_y_last_b(1)
    scatter_y_pass_a(0)
    gather_y_pass_up(0)
    scatter_y_last_a(1)
    scatter_y_pass_b(0)
    scatter_z_pass_a()
    scatter_y_last_b(3)
    gather_y_pass_down(3)
    scatter_z_pass_b()
    scatter_y_near(0)
    gather_y_pass_down(2)
    gather_y_pass_up(2)
    gather_y_pass_up(3)
    load_adam()
    gather_y_pass_down(1)
    scatter_y_last_a(0)
    gather_y_pass_up(1)
    scatter_y_last_b(0)
    adam(0, 0)
    adam(1, 0)
    gather_y_last(0)
    adam(0, 1)
    adam(1, 1)
    store_moments()
    gather_y_last(2)
    gather_y_last(3)
    forward(0, 2)
    forward(0, 0)
    gather_y_last(1)
    forward(0, 1)
    forward(0, 3)
    forward_other(3)
    forward_other(2)
    drain()
    mix(1, 0)
    forward_other(0)
    forward_other(1)
    mix(0, 0)
    store_mixed(0)
    store_kv()
    mix(0, 1)
    mix(1, 1)
    store_mixed(1)
    all_left("gossip", local)
    for copy in stores:
        copy.wait()


PIECES = 2
def finish_kernel(*refs):
    count = (len(refs) - 1) // 2
    moves = [pltpu.make_async_copy(refs[i], refs[count + i], refs[-1].at[i]) for i in range(count)]
    for move in moves:
        move.start()
    for move in moves:
        move.wait()


def finish(*arrays):
    return pl.pallas_call(
        finish_kernel,
        out_shape=tuple(jax.ShapeDtypeStruct(array.shape, array.dtype) for array in arrays),
        in_specs=[pl.BlockSpec(memory_space=pl.ANY)] * len(arrays),
        out_specs=(pl.BlockSpec(memory_space=pl.ANY),) * len(arrays),
        scratch_shapes=[pltpu.SemaphoreType.DMA((len(arrays),))],
    )(*arrays)


N_LEAVING = 13
N_ARRIVING = 6 - 1 + 3 * 4 + 4 + 4 + 4 * 4 + 4 + 4 * PIECES


def solution(mesh):
    groups = mesh.shape["gossip"]

    def body(activations, cotangent, weights, first_moment, second_moment, step_number):
        tokens, width = activations.shape[1:]
        rows, cols = weights.shape[1:]

        def call(distance, number):
            def run(step, *arrays):
                return pl.pallas_call(
                    functools.partial(kernel, distance, groups),
                    out_shape=(
                        jax.ShapeDtypeStruct((1, tokens, cols), BF16),
                        jax.ShapeDtypeStruct((1, rows, cols), BF16),
                        jax.ShapeDtypeStruct((1, rows, cols), F32),
                        jax.ShapeDtypeStruct((1, rows, cols), F32),
                    ),
                    in_specs=[pl.BlockSpec(memory_space=pl.ANY)] * 6,
                    out_specs=(pl.BlockSpec(memory_space=pl.ANY),) * 4,
                    scratch_shapes=[
                        pltpu.VMEM((tokens, width), BF16),
                        pltpu.VMEM((tokens, cols), BF16),
                        pltpu.VMEM((cols, tokens), BF16),
                        pltpu.VMEM((NC, NZ, NY, rows, cols), BF16),
                        pltpu.VMEM((NC, NZ, NY, cols, rows), BF16),
                        pltpu.VMEM((NZ, NY, cols, rows), BF16),
                        pltpu.VMEM((NZ, 6, cols // 2, rows), BF16),
                        pltpu.VMEM((6, cols // 2, rows), BF16),
                        pltpu.VMEM((rows, cols), F32),
                        pltpu.VMEM((rows, cols), F32),
                        pltpu.VMEM((rows, cols), BF16),
                        pltpu.VMEM((tokens, cols), F32),
                        pltpu.VMEM((tokens, cols), BF16),
                        pltpu.VMEM((2, rows, cols // 2), BF16),
                        pltpu.VMEM((2, rows, cols // 2), BF16),
                        pltpu.VMEM((rows, cols), BF16),
                        pltpu.SMEM((1,), jnp.int32),
                        pltpu.SemaphoreType.DMA((10,)),
                        pltpu.SemaphoreType.DMA((N_LEAVING,)),
                        pltpu.SemaphoreType.DMA((N_ARRIVING,)),
                        pltpu.SemaphoreType.DMA((3 + PIECES,)),
                    ],
                    compiler_params=pltpu.CompilerParams(
                        collective_id=number, has_side_effects=True, vmem_limit_bytes=VMEM_BYTES
                    ),
                )(step, *arrays)

            return run

        branches = [call(1 << hop, hop) for hop in range(3)]
        results = lax.switch(
            step_number[0] % 3, branches,
            step_number, activations, cotangent, weights, first_moment, second_moment,
        )
        return finish(*results)

    spread = P("gossip", "fsdp", None)
    return jax.shard_map(
        body,
        mesh=mesh,
        in_specs=(spread,) * 5 + (P(),),
        out_specs=(spread,) * 4,
        check_vma=False,
    )
```

```python
import functools

import jax
import jax.numpy as jnp
from jax import lax
from jax.experimental import pallas as pl
from jax.experimental.pallas import tpu as pltpu
from jax.sharding import PartitionSpec as P

MESH = pl.DeviceIdType.MESH
BF16 = jnp.bfloat16
F32 = jnp.float32
beta_one = 0.9
beta_two = 0.95
learn_rate = 0.001
epsilon = 1e-08
NZ, NY, NC = 4, 4, 2
ORDER = (2, 1, 3, 0)
VMEM_BYTES = 48 * 1024 * 1024


def power_of(base, exponent):
    result = jnp.float32(1.0)
    for bit in range(5):
        factor = jnp.float32(base ** (1 << bit))
        result = result * jnp.where((exponent >> bit) & 1 == 1, factor, jnp.float32(1.0))
    return result


def kernel(
    distance, groups,
    step_hbm, act_hbm, cot_hbm, w_hbm, m_hbm, v_hbm,
    kv_out, nw_out, nf_out, ns_out,
    act, cot, cot_t, wts, part, from_core, y_in, z_in, mom1, mom2, own_w, total, kv, local, peer, mixed, step_ref,
    load_sem, send_sem, recv_sem, store_sem,
):
    group, index = lax.axis_index("gossip"), lax.axis_index("fsdp")
    zi, yi, ci = index // (NY * NC), (index // NC) % NY, index % NC
    rows = w_hbm.shape[1]
    cols = w_hbm.shape[2]
    half = cols // 2

    def place(zr, yr, cr):
        return ((zi + zr) % NZ) * (NY * NC) + ((yi + yr) % NY) * NC + (ci + cr) % NC

    up_z, down_z = (group, place(1, 0, 0)), (group, place(3, 0, 0))
    up_y, down_y = (group, place(0, 1, 0)), (group, place(0, 3, 0))
    other = (group, place(0, 0, 1))
    to_peer = ((group + distance) % groups, index)
    of_peer = ((group + groups - distance) % groups, index)

    barrier = pltpu.get_barrier_semaphore()
    for device in (up_z, down_z, up_y, down_y, other, to_peer, of_peer):
        pl.semaphore_signal(barrier, inc=1, device_id=device, device_id_type=MESH)

    loads = {}

    def load(name, source, target):
        loads[name] = pltpu.make_async_copy(source, target, load_sem.at[len(loads)])
        loads[name].start()

    waited = set()

    def loaded(name):
        if name not in waited:
            waited.add(name)
            loads[name].wait()

    span = rows * NY * NC
    load("w", w_hbm.at[0], wts.at[0, 0, 0])
    load("cot", cot_hbm.at[0], cot)
    for zr in ORDER:
        window = pl.ds(pl.multiple_of(((zi + zr) % NZ) * span, span), span)
        load(("act", zr), act_hbm.at[0, :, window], act.at[:, window])
    load("m", m_hbm.at[0], mom1)
    load("v", v_hbm.at[0], mom2)
    load("own_w", w_hbm.at[0], own_w)
    load("step", step_hbm, step_ref)

    copies = {}

    leaving, arriving = {}, {}

    def describe(source, target, device, leave, arrive):
        return pltpu.make_async_remote_copy(
            src_ref=source,
            dst_ref=target,
            send_sem=send_sem.at[leaving.setdefault(leave, len(leaving))],
            recv_sem=recv_sem.at[arriving.setdefault(arrive, len(arriving))],
            device_id=device,
            device_id_type=MESH,
        )

    def prepare(name, source, target, device, leave, arrive=None):
        copies[name] = describe(source, target, device, leave, name if arrive is None else arrive)

    def send(name, source, target, device, leave, arrive=None):
        prepare(name, source, target, device, leave, arrive)
        copies[name].start()

    def arrived(name):
        copies[name].wait_recv()

    def all_arrived(arrive, whole):
        describe(whole, whole, other, next(iter(leaving)), arrive).wait_recv()

    def all_left(leave, whole):
        describe(whole, whole, other, leave, next(iter(arriving))).wait_send()

    top, low = pl.ds(0, rows // 2), pl.ds(rows // 2, rows // 2)

    def gather_core(zr, yr):
        own = w_hbm.at[0] if zr == yr == 0 else wts.at[0, zr, yr]
        send(("gc", zr, yr), own, wts.at[1, zr, yr], other, "gc", ("gcs", zr))

    def gather_y(zr):
        if zr == 3:
            arrived("gz+b")
        if zr == 1:
            arrived("gz-a")
        if zr == 2:
            all_arrived("gzp", wts.at[0, 2, 0])
        own = w_hbm.at[0] if zr == 0 else wts.at[0, zr, 0]
        send(("gy+", zr), own, wts.at[0, zr, 3], up_y, ("gy", zr))
        send(("gy-", zr), own, wts.at[0, zr, 1], down_y, ("gy", zr))
        gather_core(zr, 0)

    def gather_y_pass_up(zr):
        arrived(("gy+", zr))
        send(("gyp+", zr), wts.at[0, zr, 3, top], wts.at[0, zr, 2, top], up_y, ("gy", zr), ("gyp", zr))
        gather_core(zr, 3)

    def gather_y_pass_down(zr):
        arrived(("gy-", zr))
        send(("gyp-", zr), wts.at[0, zr, 1, low], wts.at[0, zr, 2, low], down_y, ("gy", zr), ("gyp", zr))
        gather_core(zr, 1)

    def gather_y_last(zr):
        all_arrived(("gyp", zr), wts.at[0, zr, 2])
        gather_core(zr, 2)

    def block(zr, yr, cr):
        return pl.ds(pl.multiple_of(place(zr, yr, cr) * rows, rows), rows)

    def gradient(cr, zr):
        loaded(("act", zr))
        for yr in range(NY):
            product = jnp.dot(cot_t[...], act[:, block(zr, yr, cr)], preferred_element_type=F32)
            part[cr, zr, yr] = product.astype(BF16)

    def send_other(zr):
        send(("rc", zr), part.at[1, zr], from_core.at[zr], other, "rc")

    first, second = pl.ds(0, half), pl.ds(half, half)

    def add_into(zr, yr, window, other_term):
        part[0, zr, yr, window] = part[0, zr, yr, window] + other_term

    def add_three(a, b, c):
        return a.astype(F32) + b.astype(F32) + c.astype(F32)

    def scatter_y(zr):
        arrived(("rc", zr))
        for yr in (2, 1, 3, 0):
            part[0, zr, yr] = part[0, zr, yr] + from_core[zr, yr]
        send(("y1a", zr), part.at[0, zr, 2, first], y_in.at[zr, 0], up_y, ("y", zr))
        send(("y1b", zr), part.at[0, zr, 2, second], y_in.at[zr, 1], down_y, ("y", zr))

    def scatter_y_near(zr):
        send(("y2b", zr), part.at[0, zr, 1, second], y_in.at[zr, 4], up_y, ("y", zr), ("yb", zr))
        send(("y2a", zr), part.at[0, zr, 3, first], y_in.at[zr, 2], down_y, ("y", zr), ("ya", zr))

    def scatter_y_pass_a(zr):
        arrived(("y1a", zr))
        add_into(zr, 1, first, y_in[zr, 0])
        send(("y3a", zr), part.at[0, zr, 1, first], y_in.at[zr, 3], up_y, ("y", zr), ("ya", zr))

    def scatter_y_pass_b(zr):
        arrived(("y1b", zr))
        add_into(zr, 3, second, y_in[zr, 1])
        send(("y3b", zr), part.at[0, zr, 3, second], y_in.at[zr, 5], down_y, ("y", zr), ("yb", zr))

    def reduced(zr, window):
        return part.at[0, zr, 0, window]

    def scatter_y_last_a(zr):
        all_arrived(("ya", zr), y_in.at[zr, pl.ds(2, 2)])
        part[0, zr, 0, first] = add_three(part[0, zr, 0, first], y_in[zr, 2], y_in[zr, 3]).astype(BF16)
        if zr == 2:
            send("z1a", reduced(2, first), z_in.at[0], up_z, "z")
        if zr == 3:
            send("z2a", reduced(3, first), z_in.at[3], down_z, "z")

    def scatter_y_last_b(zr):
        all_arrived(("yb", zr), y_in.at[zr, pl.ds(4, 2)])
        part[0, zr, 0, second] = add_three(part[0, zr, 0, second], y_in[zr, 4], y_in[zr, 5]).astype(BF16)
        if zr == 2:
            send("z1b", reduced(2, second), z_in.at[1], down_z, "z")
        if zr == 1:
            send("z2b", reduced(1, second), z_in.at[2], up_z, "z")

    pieces = [pl.ds(piece * (rows // PIECES), rows // PIECES) for piece in range(PIECES)]

    def scatter_z_pass_a():
        arrived("z1a")
        add_into(1, 0, first, z_in[0])
        for piece, lanes in enumerate(pieces):
            send(("z3a", piece), part.at[0, 1, 0, first, lanes], z_in.at[4, :, lanes], up_z, "z")

    def scatter_z_pass_b():
        arrived("z1b")
        add_into(3, 0, second, z_in[1])
        for piece, lanes in enumerate(pieces):
            send(("z3b", piece), part.at[0, 3, 0, second, lanes], z_in.at[5, :, lanes], down_z, "z")

    def forward(cr, zr):
        loaded("w")
        products = [
            jnp.dot(act[:, block(zr, yr, cr)], wts[cr, zr, yr], preferred_element_type=F32) for yr in range(NY)
        ]
        total[...] += (products[0] + products[1]) + (products[2] + products[3])

    def forward_other(zr):
        all_arrived(("gcs", zr), wts.at[1, zr])
        forward(1, zr)

    def start():
        pl.semaphore_wait(barrier, 7)

    lane = group % 4

    def gather_z_one_early():
        mine = w_hbm.at[0]
        prepare("gz+a", mine.at[top], wts.at[0, 3, 0, top], up_z, "gz")
        prepare("gz-b", mine.at[low], wts.at[0, 1, 0, low], down_z, "gz")

        @pl.when(lane == 0)
        def _():
            copies["gz+a"].start()
            copies["gz-b"].start()

    def gather_z_one_late():
        @pl.when(lane != 0)
        def _():
            copies["gz+a"].start()
            copies["gz-b"].start()

    def gather_z_two():
        mine = w_hbm.at[0]
        send("gz+b", mine.at[low], wts.at[0, 3, 0, low], up_z, "gz")
        send("gz-a", mine.at[top], wts.at[0, 1, 0, top], down_z, "gz")

    def gather_z_pass_up():
        arrived("gz+a")
        send("gzp+", wts.at[0, 3, 0, top], wts.at[0, 2, 0, top], up_z, "gz", "gzp")

    def gather_z_pass_down():
        arrived("gz-b")
        send("gzp-", wts.at[0, 1, 0, low], wts.at[0, 2, 0, low], down_z, "gz", "gzp")

    def turn():
        loaded("cot")
        cot_t[...] = cot[...].T

    def clear():
        total[...] = jnp.zeros_like(total)

    stores = []

    def store(source, target):
        copy = pltpu.make_async_copy(source, target, store_sem.at[len(stores)])
        copy.start()
        stores.append(copy)

    scales = []

    def load_adam():
        for name in ("m", "v", "own_w", "step"):
            loaded(name)
        count = step_ref[0] + 1
        ones = jnp.ones((1, half), F32)
        scales.append(learn_rate / (ones * (1.0 - power_of(beta_one, count))))
        scales.append(1.0 / (ones * (1.0 - power_of(beta_two, count))))

    def adam(side, piece):
        cols_at, lanes = (first, second)[side], pieces[piece]
        pure, summed, name = ((3, 4, "a"), (2, 5, "b"))[side]
        if piece == 0:
            arrived("z2" + name)
        arrived(("z3" + name, piece))
        scale_one, scale_two = scales
        gradient_t = add_three(part[0, 0, 0, cols_at, lanes], z_in[pure, :, lanes], z_in[summed, :, lanes])
        grad = gradient_t.T
        next_one = beta_one * mom1[lanes, cols_at] + (1.0 - beta_one) * grad
        next_two = beta_two * mom2[lanes, cols_at] + (1.0 - beta_two) * grad * grad
        mom1[lanes, cols_at] = next_one
        mom2[lanes, cols_at] = next_two
        update = next_one * scale_one / (jnp.sqrt(next_two * scale_two) + epsilon)
        local[side, lanes] = (own_w[lanes, cols_at].astype(F32) - update).astype(BF16)
        send(("gossip", side, piece), local.at[side, lanes], peer.at[side, lanes], to_peer, "gossip")

    def store_moments():
        store(mom1, nf_out.at[0])
        store(mom2, ns_out.at[0])

    def store_kv():
        kv[...] = total[...].astype(BF16)
        store(kv, kv_out.at[0])

    def drain():
        all_left("gz", y_in.at[0])
        for zr in range(NZ):
            all_left(("gy", zr), y_in.at[zr])
            all_left(("y", zr), y_in.at[zr])
        all_left("gc", wts.at[1])
        all_left("rc", from_core)
        all_left("z", z_in)

    def mix(side, piece):
        cols_at, lanes = (first, second)[side], pieces[piece]
        arrived(("gossip", side, piece))
        average = (local[side, lanes].astype(F32) + peer[side, lanes].astype(F32)) * 0.5
        mixed[lanes, cols_at] = average.astype(BF16)

    def store_mixed(piece):
        store(mixed.at[pieces[piece]], nw_out.at[0, pieces[piece]])

    start()
    gather_z_one_early()
    gather_y(0)
    gather_z_one_late()
    turn()
    gradient(0, 1)
    gradient(0, 2)
    gradient(1, 2)
    gradient(1, 3)
    gradient(1, 1)
    clear()
    send_other(2)
    send_other(1)
    scatter_y(2)
    gradient(1, 0)
    gradient(0, 3)
    send_other(3)
    scatter_y(1)
    gather_z_two()
    scatter_y_near(2)
    scatter_y(3)
    send_other(0)
    scatter_y_pass_a(2)
    scatter_y_pass_b(2)
    gather_z_pass_down()
    gradient(0, 0)
    scatter_y_near(3)
    gather_z_pass_up()
    scatter_y_near(1)
    scatter_y_pass_a(3)
    scatter_y_pass_b(3)
    scatter_y_pass_a(1)
    scatter_y(0)
    scatter_y_last_a(2)
    scatter_y_pass_b(1)
    scatter_y_last_b(2)
    gather_y(1)
    gather_y(3)
    gather_y_pass_down(0)
    scatter_y_last_a(3)
    scatter_y_last_b(1)
    scatter_y_pass_a(0)
    gather_y_pass_up(0)
    scatter_y_last_a(1)
    scatter_y_pass_b(0)
    scatter_y_near(0)
    gather_y(2)
    scatter_z_pass_a()
    scatter_y_last_b(3)
    gather_y_pass_down(3)
    scatter_z_pass_b()
    gather_y_pass_down(2)
    gather_y_pass_up(2)
    gather_y_pass_up(3)
    load_adam()
    gather_y_pass_down(1)
    scatter_y_last_a(0)
    gather_y_pass_up(1)
    scatter_y_last_b(0)
    adam(0, 0)
    adam(1, 0)
    gather_y_last(0)
    adam(0, 1)
    adam(1, 1)
    store_moments()
    gather_y_last(2)
    gather_y_last(3)
    forward(0, 2)
    forward(0, 0)
    gather_y_last(1)
    forward(0, 1)
    forward(0, 3)
    forward_other(3)
    forward_other(2)
    drain()
    mix(1, 0)
    forward_other(0)
    forward_other(1)
    mix(0, 0)
    store_mixed(0)
    store_kv()
    mix(0, 1)
    mix(1, 1)
    store_mixed(1)
    all_left("gossip", local)
    for copy in stores:
        copy.wait()


PIECES = 2
def finish_kernel(*refs):
    count = (len(refs) - 1) // 2
    moves = [pltpu.make_async_copy(refs[i], refs[count + i], refs[-1].at[i]) for i in range(count)]
    for move in moves:
        move.start()
    for move in moves:
        move.wait()


def finish(*arrays):
    return pl.pallas_call(
        finish_kernel,
        out_shape=tuple(jax.ShapeDtypeStruct(array.shape, array.dtype) for array in arrays),
        in_specs=[pl.BlockSpec(memory_space=pl.ANY)] * len(arrays),
        out_specs=(pl.BlockSpec(memory_space=pl.ANY),) * len(arrays),
        scratch_shapes=[pltpu.SemaphoreType.DMA((len(arrays),))],
    )(*arrays)


N_LEAVING = 13
N_ARRIVING = 6 - 1 + 3 * 4 + 4 + 4 + 4 * 4 + 4 + 4 * PIECES


def solution(mesh):
    groups = mesh.shape["gossip"]

    def body(activations, cotangent, weights, first_moment, second_moment, step_number):
        tokens, width = activations.shape[1:]
        rows, cols = weights.shape[1:]

        def call(distance, number):
            def run(step, *arrays):
                return pl.pallas_call(
                    functools.partial(kernel, distance, groups),
                    out_shape=(
                        jax.ShapeDtypeStruct((1, tokens, cols), BF16),
                        jax.ShapeDtypeStruct((1, rows, cols), BF16),
                        jax.ShapeDtypeStruct((1, rows, cols), F32),
                        jax.ShapeDtypeStruct((1, rows, cols), F32),
                    ),
                    in_specs=[pl.BlockSpec(memory_space=pl.ANY)] * 6,
                    out_specs=(pl.BlockSpec(memory_space=pl.ANY),) * 4,
                    scratch_shapes=[
                        pltpu.VMEM((tokens, width), BF16),
                        pltpu.VMEM((tokens, cols), BF16),
                        pltpu.VMEM((cols, tokens), BF16),
                        pltpu.VMEM((NC, NZ, NY, rows, cols), BF16),
                        pltpu.VMEM((NC, NZ, NY, cols, rows), BF16),
                        pltpu.VMEM((NZ, NY, cols, rows), BF16),
                        pltpu.VMEM((NZ, 6, cols // 2, rows), BF16),
                        pltpu.VMEM((6, cols // 2, rows), BF16),
                        pltpu.VMEM((rows, cols), F32),
                        pltpu.VMEM((rows, cols), F32),
                        pltpu.VMEM((rows, cols), BF16),
                        pltpu.VMEM((tokens, cols), F32),
                        pltpu.VMEM((tokens, cols), BF16),
                        pltpu.VMEM((2, rows, cols // 2), BF16),
                        pltpu.VMEM((2, rows, cols // 2), BF16),
                        pltpu.VMEM((rows, cols), BF16),
                        pltpu.SMEM((1,), jnp.int32),
                        pltpu.SemaphoreType.DMA((10,)),
                        pltpu.SemaphoreType.DMA((N_LEAVING,)),
                        pltpu.SemaphoreType.DMA((N_ARRIVING,)),
                        pltpu.SemaphoreType.DMA((3 + PIECES,)),
                    ],
                    compiler_params=pltpu.CompilerParams(
                        collective_id=number, has_side_effects=True, vmem_limit_bytes=VMEM_BYTES
                    ),
                )(step, *arrays)

            return run

        branches = [call(1 << hop, hop) for hop in range(3)]
        results = lax.switch(
            step_number[0] % 3, branches,
            step_number, activations, cotangent, weights, first_moment, second_moment,
        )
        return finish(*results)

    spread = P("gossip", "fsdp", None)
    return jax.shard_map(
        body,
        mesh=mesh,
        in_specs=(spread,) * 5 + (P(),),
        out_specs=(spread,) * 4,
        check_vma=False,
    )
```
